32 devices in a mesh: group: 1, tm: 16 (over z, y, core), head: 2 (over x), sub: 1.
Axes of the slice: x: 2, y: 2, z: 4, core: 2. Of those that a mesh axis runs over, the one named last changes fastest.
Arguments:
- queries: bfloat16 [4096, 3072], P(('group', 'tm'), ('head', 'sub')), may hold values from -12 to 12
- keys_in: bfloat16 [4096, 3072], P(('group', 'tm'), ('head', 'sub')), may hold values from -12 to 12
- values_in: bfloat16 [4096, 3072], P(('group', 'tm'), ('head', 'sub')), may hold values from -6 to 6
- out_grad: bfloat16 [4096, 3072], P(('group', 'tm'), ('head', 'sub')), may hold values from -6 to 6
- band_mask: int32 [32, 6], P('tm'), may hold values from 0 to 1, as said below
- far_tiles: int32 [16, 16], replicated, may hold values from 0 to 1
Outputs:
- attended: bfloat16 [4096, 3072], P(('group', 'tm'), ('head', 'sub'))
- query_grad: bfloat16 [4096, 3072], P(('group', 'tm'), ('head', 'sub'))
- key_grad: bfloat16 [4096, 3072], P(('group', 'tm'), ('head', 'sub'))
- value_grad: bfloat16 [4096, 3072], P(('group', 'tm'), ('head', 'sub'))
The draws below stay inside these ranges and needn't reach their ends.
Inputs may be any that keep to these rules, and one draw needn't show every extreme that they name: `band_mask`: row t and column w refer to query tile t and window tile w of t's block; the entry of t's own tile is always 1. `far_tiles`: entries are read only where the two blocks lie a power of two from 1 up apart.
All inputs are finite; a program needn't handle non-finite values.
Results may differ from the reference program's by a relative error of at most 0.023.
Values may be sent and summed in bfloat16 or wider, within the bound.
A program may use at most 128 MiB of HBM per device.

```python
import math
import jax
import jax.numpy as jnp
from jax import lax

HEADS = 24
D_HEAD = 128
TILE = 128
HALO = 256
TOK_DEV = 256
BLOCKS = 16
TOKENS = 4096
TILES = 2
WIN = 6


def draw_queries(key, part):
    normal_draw = jax.random.normal(jax.random.fold_in(key, 1), (TOKENS, HEADS * D_HEAD), jnp.float32)
    normal_draw = jnp.clip(normal_draw, -6.0, 6.0)
    return normal_draw.astype(jnp.bfloat16)


def draw_keys_in(key, part):
    normal_draw = jax.random.normal(jax.random.fold_in(key, 2), (TOKENS, HEADS * D_HEAD), jnp.float32)
    normal_draw = jnp.clip(normal_draw, -6.0, 6.0)
    return normal_draw.astype(jnp.bfloat16)


def draw_band_mask(key, part):
    tile_count = TOK_DEV // TILE
    halo_tiles = HALO // TILE
    query_tile = (jnp.arange(BLOCKS * tile_count, dtype=jnp.int32) % tile_count)[:, None]
    window_tile = jnp.arange(WIN, dtype=jnp.int32)[None, :]
    distance = jnp.abs(window_tile - halo_tiles - query_tile)
    threshold = jnp.maximum(1, 7 - 2 * distance)
    rolled = jax.random.randint(jax.random.fold_in(key, 3), (BLOCKS * tile_count, WIN), 0, 8)
    return jnp.where(distance == 0, 1, jnp.where(rolled < threshold, 1, 0)).astype(jnp.int32)


def place_ends(values, stream_key, low, top_value):
    dims = values.shape
    spot = [jax.random.randint(jax.random.fold_in(stream_key, axis), (), 0, dims[axis]) for axis in range(len(dims))]
    values = values.at[tuple(spot)].set(low)
    longest = dims.index(max(dims))
    spot[longest] = (spot[longest] + 1) % dims[longest]
    return values.at[tuple(spot)].set(top_value)


def steps_of(rng, dims, shards, smallest, top_value):
    gain, own = 1.0, jax.random.fold_in(rng, 6)
    for axis_at, shards_of in shards:
        draws = jnp.exp(jax.random.uniform(jax.random.fold_in(own, axis_at), (shards_of,), jnp.float32, smallest / len(shards), top_value / len(shards)))
        gain = gain * jnp.repeat(draws, dims[axis_at] // shards_of).reshape([-1 if axis == axis_at else 1 for axis in range(len(dims))])
    return gain


def gaussian(rng, dims, width, bound, shards=(), kind=jnp.bfloat16):
    gain = steps_of(rng, dims, shards, -0.22, 0.18) if shards else 1.0
    values = jax.random.normal(rng, dims, jnp.float32) * width * gain
    return jnp.minimum(jnp.maximum(values, -bound), bound).astype(kind)


def setup_inputs(seed: int = 0, part: int = 0) -> dict:
    splits = jax.random.split(jax.random.key(seed), 7)
    own_keys = jax.random.split(jax.random.fold_in(splits[6], part), 7)
    return {
        "queries": draw_queries(jax.random.fold_in(jax.random.fold_in(splits[6], part), 71), part),
        "keys_in": draw_keys_in(jax.random.fold_in(jax.random.fold_in(splits[6], part), 71), part),
        "values_in": gaussian(own_keys[2], (TOKENS, HEADS * D_HEAD), 1.0, 6.0, ((0, 16), (1, 2))),
        "out_grad": gaussian(own_keys[3], (TOKENS, HEADS * D_HEAD), 1.0, 6.0, ((0, 16), (1, 2))),
        "band_mask": draw_band_mask(jax.random.fold_in(splits[6], 71), part),
        "far_tiles": place_ends(jax.random.randint(splits[5], (BLOCKS, BLOCKS), 0, TILES), jax.random.fold_in(splits[5], 1), 0, TILES - 1).astype(jnp.int32),
    }


def far_offsets(count):
    offsets = []
    for level in range(0, 8):
        stride = 2 ** level
        if stride < count:
            offsets = offsets + [stride, -stride]
    return offsets

def reference(queries, keys_in, values_in, out_grad, band_mask, far_tiles):
    score_scale = 1.0 / math.sqrt(D_HEAD)
    head_cols = HEADS * D_HEAD
    offset_list = far_offsets(BLOCKS)
    far_slots = len(offset_list)
    offsets = jnp.array(offset_list, dtype=jnp.int32)
    tile_count = TOK_DEV // TILE
    halo_tiles = HALO // TILE
    window_tiles = tile_count + 2 * halo_tiles
    window_rows = TOK_DEV + 2 * HALO
    keys_padded = jnp.pad(keys_in, ((HALO, HALO), (0, 0)))
    values_padded = jnp.pad(values_in, ((HALO, HALO), (0, 0)))
    block_ids = jnp.arange(BLOCKS, dtype=jnp.int32)
    sources = block_ids[:, None] - offsets[None, :]
    source_live = (sources >= 0) & (sources < BLOCKS)
    clipped = jnp.clip(sources, 0, BLOCKS - 1).astype(jnp.int32)
    chosen = jnp.take_along_axis(far_tiles, clipped, axis=1).astype(jnp.int32)
    far_rows = (clipped * TOK_DEV + chosen * TILE)[:, :, None] + jnp.arange(TILE, dtype=jnp.int32)[None, None, :]
    far_rows = far_rows.reshape(BLOCKS, far_slots * TILE).astype(jnp.int32)

    def per_block(packed):
        index, rows_far, live_far = packed
        start = (index * TOK_DEV).astype(jnp.int32)
        query_block = lax.dynamic_slice_in_dim(queries, start, TOK_DEV, 0)
        grad_block = lax.dynamic_slice_in_dim(out_grad, start, TOK_DEV, 0)
        key_window = lax.dynamic_slice_in_dim(keys_padded, start, window_rows, 0)
        value_window = lax.dynamic_slice_in_dim(values_padded, start, window_rows, 0)
        key_set = jnp.concatenate([key_window, keys_in[rows_far]], axis=0)
        value_set = jnp.concatenate([value_window, values_in[rows_far]], axis=0)
        band = lax.dynamic_slice_in_dim(band_mask, (index * tile_count).astype(jnp.int32), tile_count, 0)
        global_tiles = index * tile_count - halo_tiles + jnp.arange(window_tiles, dtype=jnp.int32)
        inside = (global_tiles >= 0) & (global_tiles < BLOCKS * tile_count)
        tile_live = (band != 0) & inside[None, :]
        full_live = jnp.concatenate([tile_live, jnp.broadcast_to(live_far[None, :], (tile_count, far_slots))], axis=1)
        live_mask = jnp.repeat(jnp.repeat(full_live, TILE, axis=0), TILE, axis=1)
        query_cube = query_block.reshape(TOK_DEV, HEADS, D_HEAD).astype(jnp.float32)
        key_cube = key_set.reshape(-1, HEADS, D_HEAD).astype(jnp.float32)
        value_cube = value_set.reshape(-1, HEADS, D_HEAD).astype(jnp.float32)
        grad_cube = grad_block.reshape(TOK_DEV, HEADS, D_HEAD).astype(jnp.float32)
        scores = jnp.einsum('qhd,khd->hqk', query_cube, key_cube) * score_scale
        scores = jnp.where(live_mask[None, :, :], scores, -1e+30)
        top_score = lax.optimization_barrier(jnp.max(scores, axis=-1, keepdims=True))
        raised = jnp.exp(scores - top_score)
        weights = raised / lax.optimization_barrier(jnp.sum(raised, axis=-1, keepdims=True))
        weights_b = weights.astype(jnp.bfloat16)
        output = jnp.einsum('hqk,khd->qhd', weights_b.astype(jnp.float32), value_cube)
        attended_block = output.reshape(TOK_DEV, head_cols).astype(jnp.bfloat16)
        dweights = jnp.einsum('qhd,khd->hqk', grad_cube, value_cube)
        rounded_out = attended_block.reshape(TOK_DEV, HEADS, D_HEAD).astype(jnp.float32)
        row_delta = lax.optimization_barrier(jnp.sum(grad_cube * rounded_out, axis=-1))
        row_delta = jnp.transpose(row_delta, (1, 0))[:, :, None]
        dscores = (weights * (dweights - row_delta)).astype(jnp.bfloat16).astype(jnp.float32)
        query_part = jnp.einsum('hqk,khd->qhd', dscores, key_cube) * score_scale
        key_terms = jnp.einsum('hqk,qhd->khd', dscores, query_cube) * score_scale
        value_terms = jnp.einsum('hqk,qhd->khd', weights_b.astype(jnp.float32), grad_cube)
        return (attended_block, query_part.reshape(TOK_DEV, head_cols).astype(jnp.bfloat16), key_terms.reshape(-1, head_cols), value_terms.reshape(-1, head_cols))
    attended, query_grad, key_terms, value_terms = lax.map(per_block, (block_ids, far_rows, source_live))
    window_index = block_ids[:, None] * TOK_DEV + jnp.arange(window_rows, dtype=jnp.int32)[None, :]
    target_rows = jnp.concatenate([window_index, far_rows + HALO], axis=1).reshape(-1).astype(jnp.int32)
    key_total = jnp.zeros((TOKENS + 2 * HALO, head_cols), jnp.float32).at[target_rows].add(key_terms.reshape(-1, head_cols))
    value_total = jnp.zeros((TOKENS + 2 * HALO, head_cols), jnp.float32).at[target_rows].add(value_terms.reshape(-1, head_cols))
    key_grad = key_total[HALO:HALO + TOKENS].astype(jnp.bfloat16)
    value_grad = value_total[HALO:HALO + TOKENS].astype(jnp.bfloat16)
    return (attended.reshape(TOKENS, head_cols), query_grad.reshape(TOKENS, head_cols), key_grad, value_grad)
```

```python
import functools
import math

import jax
import jax.numpy as jnp
from jax import lax
from jax.experimental import pallas as pl
from jax.experimental.pallas import tpu as pltpu
from jax.sharding import PartitionSpec as P

D_HEAD = 128
TILE = 128
MESH = pl.DeviceIdType.MESH


def far_strides(count):
    strides = []
    stride = 2
    while stride < count:
        strides += [stride, -stride]
        stride *= 2
    return strides


def kernel(
    n, chunk, q_ref, k_ref, v_ref, g_ref, band_ref, far_ref, o_ref, dq_ref, dk_ref, dv_ref,
    kv, picked, bias, marks, own, gsend, grecv, send_sem, recv_sem, gsend_sem, grecv_sem,
):
    tok, cols_all = q_ref.shape
    heads = cols_all // D_HEAD
    chunks = heads // chunk
    width = 2 * D_HEAD * chunk
    tiles = tok // TILE
    rows = kv.shape[0]
    pos = lax.axis_index("tm")
    scale = 1.0 / math.sqrt(D_HEAD)
    far = far_strides(n)
    slots = [(1, tok, tok), (-1, 2 * tok, tok)]
    slots += [(d, 3 * tok + j * TILE, TILE) for j, d in enumerate(far)]
    order = list(range(len(slots)))[::-1]

    def within(index):
        return (index >= 0) & (index < n)

    barrier = pltpu.get_barrier_semaphore()
    partners = jnp.int32(0)
    for d, _, _ in slots:
        partners = partners + within(pos + d).astype(jnp.int32)

        @pl.when(within(pos + d))
        def _():
            pl.semaphore_signal(barrier, inc=1, device_id={"tm": pos + d}, device_id_type=MESH)

    pl.semaphore_wait(barrier, partners)

    def span(c):
        return pl.ds(pl.multiple_of(c * width, 2 * D_HEAD), width)

    def key_send(s, c):
        d, row, count = slots[s]
        if s < 2:
            src = kv.at[pl.ds(0, tok), span(c)]
        else:
            src = picked.at[pl.ds((s - 2) * TILE, TILE), span(c)]
        return pltpu.make_async_remote_copy(
            src_ref=src, dst_ref=kv.at[pl.ds(row, count), span(c)],
            send_sem=send_sem.at[s, c], recv_sem=recv_sem.at[s, c],
            device_id={"tm": pos + d}, device_id_type=MESH,
        )

    def key_recv(s, c):
        d, row, count = slots[s]
        ref = kv.at[pl.ds(row, count), span(c)]
        return pltpu.make_async_remote_copy(
            src_ref=ref, dst_ref=ref, send_sem=send_sem.at[s, c], recv_sem=recv_sem.at[s, c],
            device_id={"tm": pos - d}, device_id_type=MESH,
        )

    def grad_send(s, c):
        d, row, count = slots[s]
        at = pl.ds(row - tok, count)
        return pltpu.make_async_remote_copy(
            src_ref=gsend.at[at, span(c)], dst_ref=grecv.at[at, span(c)],
            send_sem=gsend_sem.at[s, c], recv_sem=grecv_sem.at[s, c],
            device_id={"tm": pos - d}, device_id_type=MESH,
        )

    def grad_recv(s, c):
        d, row, count = slots[s]
        ref = grecv.at[pl.ds(row - tok, count), span(c)]
        return pltpu.make_async_remote_copy(
            src_ref=ref, dst_ref=ref, send_sem=gsend_sem.at[s, c], recv_sem=grecv_sem.at[s, c],
            device_id={"tm": pos + d}, device_id_type=MESH,
        )

    def far_entry(reader, source):
        line = far_ref[pl.ds(jnp.clip(reader, 0, n - 1), 1), :].astype(jnp.float32)
        here = lax.broadcasted_iota(jnp.int32, line.shape, 1) == jnp.clip(source, 0, n - 1)
        return jnp.sum(jnp.where(here, line, 0.0), axis=1, keepdims=True)

    for j, d in enumerate(far):
        marks[pl.ds(j, 1), :] = jnp.broadcast_to(far_entry(pos + d, pos), (1, D_HEAD))

    def pick(ref, j, cols):
        out = ref[pl.ds(0, TILE), cols].astype(jnp.float32)
        for t in range(1, tiles):
            here = jnp.broadcast_to(marks[pl.ds(j, 1), :], (TILE, D_HEAD)) == float(t)
            out = jnp.where(here, ref[pl.ds(t * TILE, TILE), cols].astype(jnp.float32), out)
        return out.astype(ref.dtype)

    def push(c, carry):
        for i in range(chunk):
            h = c * chunk + i
            narrow = pl.ds(pl.multiple_of(h * D_HEAD, D_HEAD), D_HEAD)
            k_cols = pl.ds(pl.multiple_of(h * 2 * D_HEAD, D_HEAD), D_HEAD)
            v_cols = pl.ds(pl.multiple_of(h * 2 * D_HEAD + D_HEAD, D_HEAD), D_HEAD)
            for j, d in enumerate(far):
                picked[pl.ds(j * TILE, TILE), k_cols] = pick(k_ref, j, narrow)
                picked[pl.ds(j * TILE, TILE), v_cols] = pick(v_ref, j, narrow)
            kv[pl.ds(0, tok), k_cols] = k_ref[:, narrow]
            kv[pl.ds(0, tok), v_cols] = v_ref[:, narrow]
        for s in order:
            @pl.when(within(pos + slots[s][0]))
            def _():
                key_send(s, c).start()
        return carry

    lax.fori_loop(0, chunks, push, 0)

    for d, row, count in slots:
        @pl.when(jnp.logical_not(within(pos - d)))
        def _():
            kv[pl.ds(row, count), :] = jnp.zeros((count, kv.shape[1]), kv.dtype)

    lane = lax.broadcasted_iota(jnp.int32, (1, tok), 1) // TILE

    for t in range(rows // TILE):
        if t < 3 * tiles:
            block = t // tiles
            shift = (0, -1, 1)[block]
            at = t % tiles
            window = tiles * (1 + shift) + at
            times = jnp.zeros((1, tok), jnp.float32)
            for a in range(tiles):
                on = (band_ref[a : a + 1, window : window + 1] != 0).astype(jnp.float32)
                times = jnp.where(lane == a, jnp.broadcast_to(on, (1, tok)), times)
            if block:
                extra = (far_entry(pos, pos + shift) == float(at)).astype(jnp.float32)
                times = times + jnp.broadcast_to(extra, (1, tok))
        else:
            shift = -far[t - 3 * tiles]
            times = jnp.ones((1, tok), jnp.float32)
        times = times * within(pos + shift).astype(jnp.float32)
        bias[pl.ds(t, 1), :] = jnp.where(times == 0.0, -1e30, times - 1.0)

    lines = rows // TILE

    def head(h, carry):
        narrow = pl.ds(pl.multiple_of(h * D_HEAD, D_HEAD), D_HEAD)
        k_cols = pl.ds(pl.multiple_of(h * 2 * D_HEAD, D_HEAD), D_HEAD)
        v_cols = pl.ds(pl.multiple_of(h * 2 * D_HEAD + D_HEAD, D_HEAD), D_HEAD)
        q, g = q_ref[:, narrow], g_ref[:, narrow]
        k, v = kv[:, k_cols], kv[:, v_cols]
        last = (((1,), (1,)), ((), ()))
        first = (((0,), (0,)), ((), ()))
        f32 = jnp.float32
        scores = lax.dot_general(k, q, last, preferred_element_type=f32)
        scores = scores.reshape(lines, TILE, tok) * (scale * math.log2(math.e))
        scores = (scores + bias[0:lines, :][:, None, :]).reshape(rows, tok)
        raised = jnp.exp2(scores - jnp.max(scores, axis=0, keepdims=True))
        weights = raised * (1.0 / jnp.sum(raised, axis=0, keepdims=True))
        weights_b = weights.astype(jnp.bfloat16)
        out = lax.dot_general(v, weights_b, first, preferred_element_type=f32)
        out_b = out.T.astype(jnp.bfloat16)
        o_ref[:, narrow] = out_b
        out_t = out.astype(jnp.bfloat16).astype(f32)
        delta = jnp.sum(g.astype(f32).T * out_t, axis=0, keepdims=True)
        dweights = lax.dot_general(v, g, last, preferred_element_type=f32)
        dscores = (weights * (dweights - delta)).astype(jnp.bfloat16)
        dq = lax.dot_general(k, dscores, first, preferred_element_type=f32) * scale
        dq_ref[:, narrow] = dq.T.astype(jnp.bfloat16)
        dk = jnp.dot(dscores, q, preferred_element_type=f32) * scale
        dv = jnp.dot(weights_b, g, preferred_element_type=f32)
        own[:, k_cols] = dk[:tok]
        own[:, v_cols] = dv[:tok]
        gsend[:, k_cols] = dk[tok:].astype(jnp.bfloat16)
        gsend[:, v_cols] = dv[tok:].astype(jnp.bfloat16)
        return carry

    def work(c, carry):
        for s in order:
            @pl.when(within(pos - slots[s][0]))
            def _():
                key_recv(s, c).wait_recv()

        lax.fori_loop(c * chunk, (c + 1) * chunk, head, 0)
        for s in order:
            @pl.when(within(pos - slots[s][0]))
            def _():
                grad_send(s, c).start()
        return carry

    lax.fori_loop(0, chunks, work, 0)

    for d, row, count in slots:
        @pl.when(jnp.logical_not(within(pos + d)))
        def _():
            grecv[pl.ds(row - tok, count), :] = jnp.zeros((count, grecv.shape[1]), grecv.dtype)

    def gather(c, carry):
        for s in order:
            @pl.when(within(pos + slots[s][0]))
            def _():
                grad_recv(s, c).wait_recv()

        for i in range(chunk):
            h = c * chunk + i
            narrow = pl.ds(pl.multiple_of(h * D_HEAD, D_HEAD), D_HEAD)
            for part, ref in ((0, dk_ref), (1, dv_ref)):
                cols = pl.ds(pl.multiple_of(h * 2 * D_HEAD + part * D_HEAD, D_HEAD), D_HEAD)
                for t in range(tiles):
                    at = pl.ds(t * TILE, TILE)
                    total = own[at, cols]
                    for _, row, _ in slots[:2]:
                        total = total + grecv[pl.ds(row - tok + t * TILE, TILE), cols].astype(
                            jnp.float32
                        )
                    for j, (_, row, _) in enumerate(slots[2:]):
                        here = (marks[pl.ds(j, 1), :] == float(t)).astype(jnp.float32)
                        total = total + here * grecv[pl.ds(row - tok, TILE), cols].astype(
                            jnp.float32
                        )
                    ref[at, narrow] = total.astype(jnp.bfloat16)
        return carry

    lax.fori_loop(0, chunks, gather, 0)

    def drain(c, carry):
        for s in order:
            @pl.when(within(pos + slots[s][0]))
            def _():
                key_send(s, c).wait_send()

            @pl.when(within(pos - slots[s][0]))
            def _():
                grad_send(s, c).wait_send()
        return carry

    lax.fori_loop(0, chunks, drain, 0)


def per_device(queries, keys_in, values_in, out_grad, band_mask, far_tiles):
    tok, cols = queries.shape
    heads = cols // D_HEAD
    n = lax.axis_size("tm")
    chunk = 2 if heads % 2 == 0 else 1
    chunks = heads // chunk
    slots = 2 + len(far_strides(n))
    rows = 3 * tok + (slots - 2) * TILE
    lines = -(-rows // TILE // 8) * 8
    flops = 2 * 6 * tok * rows * cols
    bf16 = jnp.bfloat16
    vmem = pl.BlockSpec(memory_space=pltpu.VMEM)
    out = jax.ShapeDtypeStruct((tok, cols), bf16)
    sems = pltpu.SemaphoreType.DMA((slots, chunks))
    return pl.pallas_call(
        functools.partial(kernel, n, chunk),
        out_shape=(out,) * 4,
        in_specs=[vmem] * 6,
        out_specs=(vmem,) * 4,
        scratch_shapes=[
            pltpu.VMEM((rows, 2 * cols), bf16),
            pltpu.VMEM((rows - 3 * tok, 2 * cols), bf16),
            pltpu.VMEM((lines, tok), jnp.float32),
            pltpu.VMEM((max(8, slots), D_HEAD), jnp.float32),
            pltpu.VMEM((tok, 2 * cols), jnp.float32),
            pltpu.VMEM((rows - tok, 2 * cols), bf16),
            pltpu.VMEM((rows - tok, 2 * cols), bf16),
            sems, sems, sems, sems,
        ],
        compiler_params=pltpu.CompilerParams(
            collective_id=0, has_side_effects=True, vmem_limit_bytes=60 * 1024 * 1024
        ),
        cost_estimate=pl.CostEstimate(
            flops=flops, bytes_accessed=16 * tok * cols, transcendentals=tok * rows * heads
        ),
    )(queries, keys_in, values_in, out_grad, band_mask, far_tiles)


def solution(mesh):
    cells = P(("group", "tm"), ("head", "sub"))
    return jax.shard_map(
        per_device,
        mesh=mesh,
        in_specs=(cells,) * 4 + (P("tm", None), P()),
        out_specs=(cells,) * 4,
        check_vma=False,
    )
```

```python
import functools
import math

import jax
import jax.numpy as jnp
from jax import lax
from jax.experimental import pallas as pl
from jax.experimental.pallas import tpu as pltpu
from jax.sharding import PartitionSpec as P

D_HEAD = 128
TILE = 128
LEAD = 3
MESH = pl.DeviceIdType.MESH


def far_strides(count):
    strides = []
    stride = 2
    while stride < count:
        strides += [stride, -stride]
        stride *= 2
    return strides


def kernel(
    n, chunk, q_ref, k_ref, v_ref, g_ref, band_ref, far_ref, o_ref, dq_ref, dk_ref, dv_ref,
    kv, picked, bias, marks, own, gsend, grecv, passed, cut, folded, joined,
    send_sem, recv_sem, gsend_sem, grecv_sem, xsend_sem, xrecv_sem,
):
    tok, cols_all = q_ref.shape
    heads = cols_all // D_HEAD
    chunks = heads // chunk
    lead = min(LEAD, chunks)
    width = 2 * D_HEAD * chunk
    tiles = tok // TILE
    rows = kv.shape[0]
    pos = lax.axis_index("tm")
    scale = 1.0 / math.sqrt(D_HEAD)
    far = far_strides(n)
    slots = [(1, tok, tok), (-1, 2 * tok, tok)]
    slots += [(d, 3 * tok + j * TILE, TILE) for j, d in enumerate(far)]
    order = list(range(len(slots)))[::-1]

    def within(index):
        return (index >= 0) & (index < n)

    odd = lax.rem(pos, 2)
    side = 1 - 2 * odd
    mate = pos + side
    cuts = within(pos - side)
    quarter = lax.rem(pos, 4)
    third, zeroth = quarter == 3, quarter == 0
    ahead = jnp.where(third, 1, -1)
    passer = third | zeroth
    passes = passer & within(pos - 4 * ahead)
    starts = passer & within(pos + 4 * ahead)
    pass_slot = jnp.where(third, 0, 1)
    cut_mark, keep_mark = len(far), len(far) + 1
    direct = [
        jnp.logical_not(third), jnp.logical_not(zeroth), odd == 0, odd == 1,
        jnp.logical_not(third), jnp.logical_not(zeroth),
    ]
    direct += [jnp.bool_(True)] * (len(slots) - 6)

    def key_out(s):
        return within(pos + slots[s][0]) & direct[s]

    def key_in(s):
        live = within(pos - slots[s][0])
        if s < 2:
            return live & (odd == 1 - s)
        return live & direct[s] if s in (4, 5) else live

    def grad_out(s):
        live = within(pos - slots[s][0])
        if s < 2:
            return live & (odd == 1 - s)
        return live & direct[s] if s in (4, 5) else live

    def grad_in(s):
        live = within(pos + slots[s][0])
        return live if s < 2 else live & direct[s]

    barrier = pltpu.get_barrier_semaphore()
    partners = jnp.int32(0)
    for d in [d for d, _, _ in slots] + [3, -3]:
        partners = partners + within(pos + d).astype(jnp.int32)

        @pl.when(within(pos + d))
        def _():
            pl.semaphore_signal(barrier, inc=1, device_id={"tm": pos + d}, device_id_type=MESH)

    pl.semaphore_wait(barrier, partners)

    def span(c):
        return pl.ds(pl.multiple_of(c * width, 2 * D_HEAD), width)

    def key_send(s, c):
        d, row, count = slots[s]
        if s < 2:
            src = kv.at[pl.ds(0, tok), span(c)]
        else:
            src = picked.at[pl.ds((s - 2) * TILE, TILE), span(c)]
        return pltpu.make_async_remote_copy(
            src_ref=src, dst_ref=kv.at[pl.ds(row, count), span(c)],
            send_sem=send_sem.at[s, c], recv_sem=recv_sem.at[s, c],
            device_id={"tm": pos + d}, device_id_type=MESH,
        )

    def key_recv(s, c):
        d, row, count = slots[s]
        ref = kv.at[pl.ds(row, count), span(c)]
        return pltpu.make_async_remote_copy(
            src_ref=ref, dst_ref=ref, send_sem=send_sem.at[s, c], recv_sem=recv_sem.at[s, c],
            device_id={"tm": pos - d}, device_id_type=MESH,
        )

    def remote(src, dst, sent, arrived, to):
        return pltpu.make_async_remote_copy(
            src_ref=src, dst_ref=dst, send_sem=sent, recv_sem=arrived,
            device_id={"tm": to}, device_id_type=MESH,
        )

    def start_send(c):
        return remote(
            kv.at[pl.ds(0, tok), span(c)], passed.at[:, span(c)],
            xsend_sem.at[3, c], xrecv_sem.at[0, c], pos + 4 * ahead,
        )

    def pass_recv(c):
        ref = passed.at[:, span(c)]
        return remote(ref, ref, xsend_sem.at[3, c], xrecv_sem.at[0, c], pos - 4 * ahead)

    def pass_send(c):
        row = pl.multiple_of(tok * (1 + pass_slot), tok)
        return remote(
            passed.at[:, span(c)], kv.at[pl.ds(row, tok), span(c)],
            xsend_sem.at[0, c], recv_sem.at[pass_slot, c], pos - 3 * ahead,
        )

    def whole_recv(c):
        ref = kv.at[pl.ds(pl.multiple_of(tok * (1 + odd), tok), tok), span(c)]
        return remote(ref, ref, send_sem.at[odd, c], recv_sem.at[odd, c], pos - side)

    def cut_send(c):
        row = pl.multiple_of(3 * tok + odd * TILE, TILE)
        return remote(
            cut.at[:, span(c)], kv.at[pl.ds(row, TILE), span(c)],
            xsend_sem.at[1, c], recv_sem.at[2 + odd, c], mate,
        )

    def fold_recv(c):
        ref = folded.at[:, span(c)]
        return remote(ref, ref, xsend_sem.at[1, c], xrecv_sem.at[1, c], mate)

    def whole_rows():
        return pl.ds(pl.multiple_of(odd * tok, tok), tok)

    def fold_send(c):
        return remote(
            gsend.at[whole_rows(), span(c)], grecv.at[whole_rows(), span(c)],
            gsend_sem.at[odd, c], grecv_sem.at[odd, c], pos - side,
        )

    def fold_send_pass(c):
        return remote(
            gsend.at[whole_rows(), span(c)], joined.at[:, span(c)],
            gsend_sem.at[odd, c], xrecv_sem.at[2, c], pos + 3 * side,
        )

    def join_recv(c):
        ref = joined.at[:, span(c)]
        return remote(ref, ref, xsend_sem.at[2, c], xrecv_sem.at[2, c], pos - 3 * ahead)

    def join_send(c):
        row = pl.multiple_of(tok * pass_slot, tok)
        return remote(
            joined.at[:, span(c)], grecv.at[pl.ds(row, tok), span(c)],
            xsend_sem.at[2, c], grecv_sem.at[pass_slot, c], pos - 4 * ahead,
        )

    def grad_send(s, c):
        d, row, count = slots[s]
        src = gsend.at[pl.ds(row - tok, count), span(c)]
        return remote(
            src, grecv.at[pl.ds(row - tok, count), span(c)],
            gsend_sem.at[s, c], grecv_sem.at[s, c], pos - d,
        )

    def mate_send(s, c):
        d, row, count = slots[s]
        src = gsend.at[pl.ds(row - tok, count), span(c)]
        return remote(
            src, folded.at[:, span(c)], gsend_sem.at[s, c], xrecv_sem.at[1, c], mate
        )

    def send_grad(s, c, action):
        if s in (2, 3):
            to_mate = odd == 3 - s

            @pl.when(grad_out(s) & to_mate)
            def _():
                action(mate_send(s, c))

            @pl.when(grad_out(s) & jnp.logical_not(to_mate))
            def _():
                action(grad_send(s, c))
        else:
            @pl.when(grad_out(s))
            def _():
                action(grad_send(s, c))

    def grad_recv(s, c):
        d, row, count = slots[s]
        ref = grecv.at[pl.ds(row - tok, count), span(c)]
        return pltpu.make_async_remote_copy(
            src_ref=ref, dst_ref=ref, send_sem=gsend_sem.at[s, c], recv_sem=grecv_sem.at[s, c],
            device_id={"tm": pos + d}, device_id_type=MESH,
        )

    def far_entry(reader, source):
        line = far_ref[pl.ds(jnp.clip(reader, 0, n - 1), 1), :].astype(jnp.float32)
        here = lax.broadcasted_iota(jnp.int32, line.shape, 1) == jnp.clip(source, 0, n - 1)
        return jnp.sum(jnp.where(here, line, 0.0), axis=1, keepdims=True)

    for j, d in enumerate(far):
        marks[pl.ds(j, 1), :] = jnp.broadcast_to(far_entry(pos + d, pos), (1, D_HEAD))

    marks[pl.ds(cut_mark, 1), :] = jnp.broadcast_to(
        far_entry(mate, pos - side), (1, D_HEAD)
    )
    marks[pl.ds(keep_mark, 1), :] = jnp.broadcast_to(
        far_entry(pos, pos - 4 * ahead), (1, D_HEAD)
    )

    def pick(ref, j, cols, base=0):
        out = None
        for t in range(tiles):
            row = base + t * TILE
            if not isinstance(row, int):
                row = pl.multiple_of(row, TILE)
            part = ref[pl.ds(row, TILE), cols].astype(jnp.float32)
            here = jnp.broadcast_to(marks[pl.ds(j, 1), :], (TILE, D_HEAD)) == float(t)
            out = part if out is None else jnp.where(here, part, out)
        return out.astype(ref.dtype)

    def add_tile(ref, base, extra, j, cols):
        for t in range(tiles):
            row = base + t * TILE
            if not isinstance(row, int):
                row = pl.multiple_of(row, TILE)
            here = (marks[pl.ds(j, 1), :] == float(t)).astype(jnp.float32)
            total = ref[pl.ds(row, TILE), cols].astype(jnp.float32) + here * extra
            ref[pl.ds(row, TILE), cols] = total.astype(ref.dtype)

    def push(c, carry):
        for i in range(chunk):
            h = c * chunk + i
            narrow = pl.ds(pl.multiple_of(h * D_HEAD, D_HEAD), D_HEAD)
            k_cols = pl.ds(pl.multiple_of(h * 2 * D_HEAD, D_HEAD), D_HEAD)
            v_cols = pl.ds(pl.multiple_of(h * 2 * D_HEAD + D_HEAD, D_HEAD), D_HEAD)
            for j, d in enumerate(far):
                picked[pl.ds(j * TILE, TILE), k_cols] = pick(k_ref, j, narrow)
                picked[pl.ds(j * TILE, TILE), v_cols] = pick(v_ref, j, narrow)
            kv[pl.ds(0, tok), k_cols] = k_ref[:, narrow]
            kv[pl.ds(0, tok), v_cols] = v_ref[:, narrow]
        @pl.when(starts)
        def _():
            start_send(c).start()

        for s in order:
            @pl.when(key_out(s))
            def _():
                key_send(s, c).start()
        return carry

    lax.fori_loop(0, lead, push, 0)

    for d, row, count in slots:
        @pl.when(jnp.logical_not(within(pos - d)))
        def _():
            kv[pl.ds(row, count), :] = jnp.zeros((count, kv.shape[1]), kv.dtype)

    lane = lax.broadcasted_iota(jnp.int32, (1, tok), 1) // TILE

    for t in range(rows // TILE):
        if t < 3 * tiles:
            block = t // tiles
            shift = (0, -1, 1)[block]
            at = t % tiles
            window = tiles * (1 + shift) + at
            times = jnp.zeros((1, tok), jnp.float32)
            for a in range(tiles):
                on = (band_ref[a : a + 1, window : window + 1] != 0).astype(jnp.float32)
                times = jnp.where(lane == a, jnp.broadcast_to(on, (1, tok)), times)
            if block:
                extra = (far_entry(pos, pos + shift) == float(at)).astype(jnp.float32)
                times = times + jnp.broadcast_to(extra, (1, tok))
        else:
            shift = -far[t - 3 * tiles]
            times = jnp.ones((1, tok), jnp.float32)
        times = times * within(pos + shift).astype(jnp.float32)
        bias[pl.ds(t, 1), :] = jnp.where(times == 0.0, -1e30, times - 1.0)

    lines = rows // TILE

    def head(h, carry):
        narrow = pl.ds(pl.multiple_of(h * D_HEAD, D_HEAD), D_HEAD)
        k_cols = pl.ds(pl.multiple_of(h * 2 * D_HEAD, D_HEAD), D_HEAD)
        v_cols = pl.ds(pl.multiple_of(h * 2 * D_HEAD + D_HEAD, D_HEAD), D_HEAD)
        q, g = q_ref[:, narrow], g_ref[:, narrow]
        k, v = kv[:, k_cols], kv[:, v_cols]
        last = (((1,), (1,)), ((), ()))
        first = (((0,), (0,)), ((), ()))
        f32 = jnp.float32
        scores = lax.dot_general(k, q, last, preferred_element_type=f32)
        scores = scores.reshape(lines, TILE, tok) * (scale * math.log2(math.e))
        scores = (scores + bias[0:lines, :][:, None, :]).reshape(rows, tok)
        raised = jnp.exp2(scores - jnp.max(scores, axis=0, keepdims=True))
        weights = raised * (1.0 / jnp.sum(raised, axis=0, keepdims=True))
        weights_b = weights.astype(jnp.bfloat16)
        out = lax.dot_general(v, weights_b, first, preferred_element_type=f32)
        out_b = out.T.astype(jnp.bfloat16)
        o_ref[:, narrow] = out_b
        out_t = out.astype(jnp.bfloat16).astype(f32)
        delta = jnp.sum(g.astype(f32).T * out_t, axis=0, keepdims=True)
        dweights = lax.dot_general(v, g, last, preferred_element_type=f32)
        dscores = (weights * (dweights - delta)).astype(jnp.bfloat16)
        dq = lax.dot_general(k, dscores, first, preferred_element_type=f32) * scale
        dq_ref[:, narrow] = dq.T.astype(jnp.bfloat16)
        dk = jnp.dot(dscores, q, preferred_element_type=f32) * scale
        dv = jnp.dot(weights_b, g, preferred_element_type=f32)
        own[:, k_cols] = dk[:tok]
        own[:, v_cols] = dv[:tok]
        gsend[:, k_cols] = dk[tok:].astype(jnp.bfloat16)
        gsend[:, v_cols] = dv[tok:].astype(jnp.bfloat16)
        return carry

    def piece(c, i):
        return pl.ds(pl.multiple_of(c * width + i * D_HEAD, D_HEAD), D_HEAD)

    def fold(c):
        @pl.when(cuts)
        def _():
            fold_recv(c).wait_recv()
            for i in range(2 * chunk):
                extra = folded[:, piece(c, i)].astype(jnp.float32)
                add_tile(gsend, odd * tok, extra, cut_mark, piece(c, i))

        @pl.when(cuts & passer)
        def _():
            fold_send_pass(c).start()

        @pl.when(cuts & jnp.logical_not(passer))
        def _():
            fold_send(c).start()

    def join(c):
        @pl.when(passes)
        def _():
            join_recv(c).wait_recv()
            row = pl.multiple_of(2 * tok + (2 + pass_slot) * TILE, TILE)
            for i in range(2 * chunk):
                extra = gsend[pl.ds(row, TILE), piece(c, i)].astype(jnp.float32)
                add_tile(joined, 0, extra, keep_mark, piece(c, i))
            join_send(c).start()

    def work(c, carry):
        @pl.when(c + lead < chunks)
        def _():
            push(c + lead, 0)

        @pl.when(passes)
        def _():
            pass_recv(c).wait_recv()
            pass_send(c).start()
            row = pl.multiple_of(3 * tok + (2 + pass_slot) * TILE, TILE)
            for i in range(2 * chunk):
                kv[pl.ds(row, TILE), piece(c, i)] = pick(passed, keep_mark, piece(c, i))

        @pl.when(cuts)
        def _():
            whole_recv(c).wait_recv()
            for i in range(2 * chunk):
                cut[:, piece(c, i)] = pick(kv, cut_mark, piece(c, i), tok * (1 + odd))
            cut_send(c).start()

        for s in order:
            @pl.when(key_in(s))
            def _():
                key_recv(s, c).wait_recv()

        lax.fori_loop(c * chunk, (c + 1) * chunk, head, 0)
        for s in order:
            send_grad(s, c, lambda copy: copy.start())

        @pl.when(c >= 1)
        def _():
            fold(c - 1)

        @pl.when(c >= 2)
        def _():
            join(c - 2)
        return carry

    lax.fori_loop(0, chunks, work, 0)
    fold(chunks - 1)
    if chunks > 1:
        join(chunks - 2)
    join(chunks - 1)

    for d, row, count in slots:
        @pl.when(jnp.logical_not(grad_in(slots.index((d, row, count)))))
        def _():
            grecv[pl.ds(row - tok, count), :] = jnp.zeros((count, grecv.shape[1]), grecv.dtype)

    def gather(c, carry):
        for s in order:
            @pl.when(grad_in(s))
            def _():
                grad_recv(s, c).wait_recv()

        for i in range(chunk):
            h = c * chunk + i
            narrow = pl.ds(pl.multiple_of(h * D_HEAD, D_HEAD), D_HEAD)
            for part, ref in ((0, dk_ref), (1, dv_ref)):
                cols = pl.ds(pl.multiple_of(h * 2 * D_HEAD + part * D_HEAD, D_HEAD), D_HEAD)
                for t in range(tiles):
                    at = pl.ds(t * TILE, TILE)
                    total = own[at, cols]
                    for _, row, _ in slots[:2]:
                        total = total + grecv[pl.ds(row - tok + t * TILE, TILE), cols].astype(
                            jnp.float32
                        )
                    for j, (_, row, _) in enumerate(slots[2:]):
                        here = (marks[pl.ds(j, 1), :] == float(t)).astype(jnp.float32)
                        total = total + here * grecv[pl.ds(row - tok, TILE), cols].astype(
                            jnp.float32
                        )
                    ref[at, narrow] = total.astype(jnp.bfloat16)
        return carry

    lax.fori_loop(0, chunks, gather, 0)

    def drain(c, carry):
        for s in order:
            @pl.when(key_out(s))
            def _():
                key_send(s, c).wait_send()

            send_grad(s, c, lambda copy: copy.wait_send())

        @pl.when(starts)
        def _():
            start_send(c).wait_send()

        @pl.when(passes)
        def _():
            pass_send(c).wait_send()
            join_send(c).wait_send()

        @pl.when(cuts)
        def _():
            cut_send(c).wait_send()

        @pl.when(cuts & passer)
        def _():
            fold_send_pass(c).wait_send()

        @pl.when(cuts & jnp.logical_not(passer))
        def _():
            fold_send(c).wait_send()
        return carry

    lax.fori_loop(0, chunks, drain, 0)


def per_device(queries, keys_in, values_in, out_grad, band_mask, far_tiles):
    tok, cols = queries.shape
    heads = cols // D_HEAD
    n = lax.axis_size("tm")
    chunk = 2 if heads % 2 == 0 else 1
    chunks = heads // chunk
    slots = 2 + len(far_strides(n))
    rows = 3 * tok + (slots - 2) * TILE
    lines = -(-rows // TILE // 8) * 8
    flops = 2 * 6 * tok * rows * cols
    bf16 = jnp.bfloat16
    vmem = pl.BlockSpec(memory_space=pltpu.VMEM)
    out = jax.ShapeDtypeStruct((tok, cols), bf16)
    sems = pltpu.SemaphoreType.DMA((slots, chunks))
    return pl.pallas_call(
        functools.partial(kernel, n, chunk),
        out_shape=(out,) * 4,
        in_specs=[vmem] * 6,
        out_specs=(vmem,) * 4,
        scratch_shapes=[
            pltpu.VMEM((rows, 2 * cols), bf16),
            pltpu.VMEM((rows - 3 * tok, 2 * cols), bf16),
            pltpu.VMEM((lines, tok), jnp.float32),
            pltpu.VMEM((16, D_HEAD), jnp.float32),
            pltpu.VMEM((tok, 2 * cols), jnp.float32),
            pltpu.VMEM((rows - tok, 2 * cols), bf16),
            pltpu.VMEM((rows - tok, 2 * cols), bf16),
            pltpu.VMEM((tok, 2 * cols), bf16),
            pltpu.VMEM((TILE, 2 * cols), bf16),
            pltpu.VMEM((TILE, 2 * cols), bf16),
            pltpu.VMEM((tok, 2 * cols), bf16),
            sems, sems, sems, sems,
            pltpu.SemaphoreType.DMA((4, chunks)),
            pltpu.SemaphoreType.DMA((3, chunks)),
        ],
        compiler_params=pltpu.CompilerParams(
            collective_id=0, has_side_effects=True, vmem_limit_bytes=60 * 1024 * 1024
        ),
        cost_estimate=pl.CostEstimate(
            flops=flops, bytes_accessed=16 * tok * cols, transcendentals=tok * rows * heads
        ),
    )(queries, keys_in, values_in, out_grad, band_mask, far_tiles)


def solution(mesh):
    cells = P(("group", "tm"), ("head", "sub"))
    return jax.shard_map(
        per_device,
        mesh=mesh,
        in_specs=(cells,) * 4 + (P("tm", None), P()),
        out_specs=(cells,) * 4,
        check_vma=False,
    )
```

```python
import functools
import math

import jax
import jax.numpy as jnp
from jax import lax
from jax.experimental import pallas as pl
from jax.experimental.pallas import tpu as pltpu
from jax.sharding import PartitionSpec as P

D_HEAD = 128
TILE = 128
LEAD = 12
MESH = pl.DeviceIdType.MESH


def far_strides(count):
    strides = []
    stride = 2
    while stride < count:
        strides += [stride, -stride]
        stride *= 2
    return strides


def kernel(
    n, chunk, q_ref, k_ref, v_ref, g_ref, band_ref, far_ref, o_ref, dq_ref, dk_ref, dv_ref,
    kv, picked, bias, marks, own, gsend, grecv, passed, cut, folded, joined,
    onward, turned, back8, back2, back,
    send_sem, recv_sem, gsend_sem, grecv_sem, xsend_sem, xrecv_sem,
):
    tok, cols_all = q_ref.shape
    heads = cols_all // D_HEAD
    chunks = heads // chunk
    lead = min(LEAD, chunks)
    width = 2 * D_HEAD * chunk
    tiles = tok // TILE
    rows = kv.shape[0]
    pos = lax.axis_index("tm")
    scale = 1.0 / math.sqrt(D_HEAD)
    far = far_strides(n)
    slots = [(1, tok, tok), (-1, 2 * tok, tok)]
    slots += [(d, 3 * tok + j * TILE, TILE) for j, d in enumerate(far)]
    order = list(range(len(slots)))[::-1]

    def within(index):
        return (index >= 0) & (index < n)

    odd = lax.rem(pos, 2)
    side = 1 - 2 * odd
    mate = pos + side
    cuts = within(pos - side)
    quarter = lax.rem(pos, 4)
    third, zeroth = quarter == 3, quarter == 0
    passer = third | zeroth
    upper = quarter >= 2
    ahead = jnp.where(upper, 1, -1)
    pass_slot = jnp.where(upper, 0, 1)
    passes = within(pos - 4 * ahead)
    starts = within(pos + 4 * ahead)
    goes_on = passes & starts
    cut_mark, keep_mark = len(far), len(far) + 1
    on_mark, turn_mark = len(far) + 2, len(far) + 3
    lower = jnp.logical_not(upper)
    direct = [
        jnp.logical_not(third), jnp.logical_not(zeroth), zeroth, third,
        lower, upper, lower, upper,
    ]
    direct += [jnp.bool_(True)] * (len(slots) - 8)

    def key_out(s):
        return within(pos + slots[s][0]) & direct[s]

    def key_in(s):
        live = within(pos - slots[s][0])
        if s < 2:
            return live & (odd == 1 - s)
        return live & direct[s] if s in (4, 5) else live

    def grad_out(s):
        live = within(pos - slots[s][0])
        if s < 2:
            return live & (odd == 1 - s)
        return live & direct[s] if s in (4, 5) else live

    def grad_in(s):
        live = within(pos + slots[s][0])
        return live & direct[s]

    barrier = pltpu.get_barrier_semaphore()
    partners = jnp.int32(0)
    for d in [d for d, _, _ in slots] + [3, -3]:
        partners = partners + within(pos + d).astype(jnp.int32)

        @pl.when(within(pos + d))
        def _():
            pl.semaphore_signal(barrier, inc=1, device_id={"tm": pos + d}, device_id_type=MESH)

    pl.semaphore_wait(barrier, partners)

    def span(c):
        return pl.ds(pl.multiple_of(c * width, 2 * D_HEAD), width)

    def key_send(s, c):
        d, row, count = slots[s]
        if s < 2:
            src = kv.at[pl.ds(0, tok), span(c)]
        else:
            src = picked.at[pl.ds((s - 2) * TILE, TILE), span(c)]
        return pltpu.make_async_remote_copy(
            src_ref=src, dst_ref=kv.at[pl.ds(row, count), span(c)],
            send_sem=send_sem.at[s, c], recv_sem=recv_sem.at[s, c],
            device_id={"tm": pos + d}, device_id_type=MESH,
        )

    def key_recv(s, c):
        d, row, count = slots[s]
        ref = kv.at[pl.ds(row, count), span(c)]
        return pltpu.make_async_remote_copy(
            src_ref=ref, dst_ref=ref, send_sem=send_sem.at[s, c], recv_sem=recv_sem.at[s, c],
            device_id={"tm": pos - d}, device_id_type=MESH,
        )

    def remote(src, dst, sent, arrived, to):
        return pltpu.make_async_remote_copy(
            src_ref=src, dst_ref=dst, send_sem=sent, recv_sem=arrived,
            device_id={"tm": to}, device_id_type=MESH,
        )

    def start_send(c):
        return remote(
            kv.at[pl.ds(0, tok), span(c)], passed.at[:, span(c)],
            xsend_sem.at[3, c], xrecv_sem.at[0, c], pos + 4 * ahead,
        )

    def pass_recv(c):
        ref = passed.at[:, span(c)]
        return remote(ref, ref, xsend_sem.at[3, c], xrecv_sem.at[0, c], pos - 4 * ahead)

    def pass_send(c):
        row = pl.multiple_of(tok * (1 + pass_slot), tok)
        return remote(
            passed.at[:, span(c)], kv.at[pl.ds(row, tok), span(c)],
            xsend_sem.at[0, c], recv_sem.at[pass_slot, c], pos - 3 * ahead,
        )

    def turn_send(c):
        row = pl.multiple_of(3 * tok + pass_slot * TILE, TILE)
        return remote(
            turned.at[:, span(c)], kv.at[pl.ds(row, TILE), span(c)],
            xsend_sem.at[4, c], recv_sem.at[2 + pass_slot, c], pos - 2 * ahead,
        )

    def on_send(c):
        row = pl.multiple_of(3 * tok + (4 + pass_slot) * TILE, TILE)
        return remote(
            onward.at[:, span(c)], kv.at[pl.ds(row, TILE), span(c)],
            xsend_sem.at[5, c], recv_sem.at[6 + pass_slot, c], pos + 4 * ahead,
        )

    def back2_recv(c):
        ref = back2.at[:, span(c)]
        return remote(ref, ref, xsend_sem.at[4, c], xrecv_sem.at[3, c], pos - 2 * ahead)

    def back8_recv(c):
        ref = back8.at[:, span(c)]
        return remote(ref, ref, xsend_sem.at[5, c], xrecv_sem.at[4, c], pos + 4 * ahead)

    def back_recv(c):
        ref = back.at[:, span(c)]
        return remote(ref, ref, xsend_sem.at[2, c], xrecv_sem.at[5, c], pos + 4 * ahead)

    def whole_recv(c):
        ref = kv.at[pl.ds(pl.multiple_of(tok * (1 + odd), tok), tok), span(c)]
        return remote(ref, ref, send_sem.at[odd, c], recv_sem.at[odd, c], pos - side)

    def cut_send(c):
        row = pl.multiple_of(3 * tok + odd * TILE, TILE)
        return remote(
            cut.at[:, span(c)], kv.at[pl.ds(row, TILE), span(c)],
            xsend_sem.at[1, c], recv_sem.at[2 + odd, c], mate,
        )

    def fold_recv(c):
        ref = folded.at[:, span(c)]
        return remote(ref, ref, xsend_sem.at[1, c], xrecv_sem.at[1, c], mate)

    def whole_rows():
        return pl.ds(pl.multiple_of(odd * tok, tok), tok)

    def fold_send(c):
        return remote(
            gsend.at[whole_rows(), span(c)], grecv.at[whole_rows(), span(c)],
            gsend_sem.at[odd, c], grecv_sem.at[odd, c], pos - side,
        )

    def fold_send_pass(c):
        return remote(
            gsend.at[whole_rows(), span(c)], joined.at[:, span(c)],
            gsend_sem.at[odd, c], xrecv_sem.at[2, c], pos + 3 * side,
        )

    def join_recv(c):
        ref = joined.at[:, span(c)]
        return remote(ref, ref, xsend_sem.at[2, c], xrecv_sem.at[2, c], pos - 3 * ahead)

    def join_send(c):
        return remote(
            joined.at[:, span(c)], back.at[:, span(c)],
            xsend_sem.at[2, c], xrecv_sem.at[5, c], pos - 4 * ahead,
        )

    def grad_send(s, c):
        d, row, count = slots[s]
        src = gsend.at[pl.ds(row - tok, count), span(c)]
        return remote(
            src, grecv.at[pl.ds(row - tok, count), span(c)],
            gsend_sem.at[s, c], grecv_sem.at[s, c], pos - d,
        )

    def mate_send(s, c):
        d, row, count = slots[s]
        src = gsend.at[pl.ds(row - tok, count), span(c)]
        return remote(
            src, folded.at[:, span(c)], gsend_sem.at[s, c], xrecv_sem.at[1, c], mate
        )

    def turn_back(s, c):
        d, row, count = slots[s]
        src = gsend.at[pl.ds(row - tok, count), span(c)]
        return remote(
            src, back2.at[:, span(c)], gsend_sem.at[s, c], xrecv_sem.at[3, c], pos + d
        )

    def on_back(s, c):
        d, row, count = slots[s]
        src = gsend.at[pl.ds(row - tok, count), span(c)]
        return remote(
            src, back8.at[:, span(c)], gsend_sem.at[s, c], xrecv_sem.at[4, c], pos - d // 2
        )

    def send_grad(s, c, action):
        never = jnp.bool_(False)
        to_mate = to_turn = to_on = never
        if s in (2, 3):
            to_mate = odd == 3 - s
            to_turn = zeroth if s == 2 else third

            @pl.when(grad_out(s) & to_mate)
            def _():
                action(mate_send(s, c))

            @pl.when(grad_out(s) & to_turn)
            def _():
                action(turn_back(s, c))
        if s in (6, 7):
            to_on = upper if s == 6 else lower

            @pl.when(grad_out(s) & to_on)
            def _():
                action(on_back(s, c))

        @pl.when(grad_out(s) & jnp.logical_not(to_mate | to_turn | to_on))
        def _():
            action(grad_send(s, c))

    def grad_recv(s, c):
        d, row, count = slots[s]
        ref = grecv.at[pl.ds(row - tok, count), span(c)]
        return pltpu.make_async_remote_copy(
            src_ref=ref, dst_ref=ref, send_sem=gsend_sem.at[s, c], recv_sem=grecv_sem.at[s, c],
            device_id={"tm": pos + d}, device_id_type=MESH,
        )

    def far_entry(reader, source):
        line = far_ref[pl.ds(jnp.clip(reader, 0, n - 1), 1), :].astype(jnp.float32)
        here = lax.broadcasted_iota(jnp.int32, line.shape, 1) == jnp.clip(source, 0, n - 1)
        return jnp.sum(jnp.where(here, line, 0.0), axis=1, keepdims=True)

    for j, d in enumerate(far):
        marks[pl.ds(j, 1), :] = jnp.broadcast_to(far_entry(pos + d, pos), (1, D_HEAD))

    marks[pl.ds(cut_mark, 1), :] = jnp.broadcast_to(
        far_entry(mate, pos - side), (1, D_HEAD)
    )
    marks[pl.ds(keep_mark, 1), :] = jnp.broadcast_to(
        far_entry(pos, pos - 4 * ahead), (1, D_HEAD)
    )
    marks[pl.ds(on_mark, 1), :] = jnp.broadcast_to(
        far_entry(pos + 4 * ahead, pos - 4 * ahead), (1, D_HEAD)
    )
    marks[pl.ds(turn_mark, 1), :] = jnp.broadcast_to(
        far_entry(pos - 2 * ahead, pos - 4 * ahead), (1, D_HEAD)
    )

    def pick(ref, j, cols, base=0):
        out = None
        for t in range(tiles):
            row = base + t * TILE
            if not isinstance(row, int):
                row = pl.multiple_of(row, TILE)
            part = ref[pl.ds(row, TILE), cols].astype(jnp.float32)
            here = jnp.broadcast_to(marks[pl.ds(j, 1), :], (TILE, D_HEAD)) == float(t)
            out = part if out is None else jnp.where(here, part, out)
        return out.astype(ref.dtype)

    def add_tile(ref, base, extra, j, cols):
        for t in range(tiles):
            row = base + t * TILE
            if not isinstance(row, int):
                row = pl.multiple_of(row, TILE)
            here = (marks[pl.ds(j, 1), :] == float(t)).astype(jnp.float32)
            total = ref[pl.ds(row, TILE), cols].astype(jnp.float32) + here * extra
            ref[pl.ds(row, TILE), cols] = total.astype(ref.dtype)

    def push(c, carry):
        for i in range(chunk):
            h = c * chunk + i
            narrow = pl.ds(pl.multiple_of(h * D_HEAD, D_HEAD), D_HEAD)
            k_cols = pl.ds(pl.multiple_of(h * 2 * D_HEAD, D_HEAD), D_HEAD)
            v_cols = pl.ds(pl.multiple_of(h * 2 * D_HEAD + D_HEAD, D_HEAD), D_HEAD)
            for j, d in enumerate(far):
                picked[pl.ds(j * TILE, TILE), k_cols] = pick(k_ref, j, narrow)
                picked[pl.ds(j * TILE, TILE), v_cols] = pick(v_ref, j, narrow)
            kv[pl.ds(0, tok), k_cols] = k_ref[:, narrow]
            kv[pl.ds(0, tok), v_cols] = v_ref[:, narrow]
        @pl.when(starts)
        def _():
            start_send(c).start()

        for s in order:
            @pl.when(key_out(s))
            def _():
                key_send(s, c).start()
        return carry

    lax.fori_loop(0, lead, push, 0)

    for d, row, count in slots:
        @pl.when(jnp.logical_not(within(pos - d)))
        def _():
            kv[pl.ds(row, count), :] = jnp.zeros((count, kv.shape[1]), kv.dtype)

    for ref, filled in (
        (joined, passes & passer), (back2, passes & jnp.logical_not(passer)),
        (back8, goes_on), (back, starts),
    ):
        @pl.when(jnp.logical_not(filled))
        def _():
            ref[...] = jnp.zeros(ref.shape, ref.dtype)

    lane = lax.broadcasted_iota(jnp.int32, (1, tok), 1) // TILE

    for t in range(rows // TILE):
        if t < 3 * tiles:
            block = t // tiles
            shift = (0, -1, 1)[block]
            at = t % tiles
            window = tiles * (1 + shift) + at
            times = jnp.zeros((1, tok), jnp.float32)
            for a in range(tiles):
                on = (band_ref[a : a + 1, window : window + 1] != 0).astype(jnp.float32)
                times = jnp.where(lane == a, jnp.broadcast_to(on, (1, tok)), times)
            if block:
                extra = (far_entry(pos, pos + shift) == float(at)).astype(jnp.float32)
                times = times + jnp.broadcast_to(extra, (1, tok))
        else:
            shift = -far[t - 3 * tiles]
            times = jnp.ones((1, tok), jnp.float32)
        times = times * within(pos + shift).astype(jnp.float32)
        bias[pl.ds(t, 1), :] = jnp.where(times == 0.0, -1e30, times - 1.0)

    lines = rows // TILE

    def head(h, carry):
        narrow = pl.ds(pl.multiple_of(h * D_HEAD, D_HEAD), D_HEAD)
        k_cols = pl.ds(pl.multiple_of(h * 2 * D_HEAD, D_HEAD), D_HEAD)
        v_cols = pl.ds(pl.multiple_of(h * 2 * D_HEAD + D_HEAD, D_HEAD), D_HEAD)
        q, g = q_ref[:, narrow], g_ref[:, narrow]
        k, v = kv[:, k_cols], kv[:, v_cols]
        last = (((1,), (1,)), ((), ()))
        first = (((0,), (0,)), ((), ()))
        f32 = jnp.float32
        scores = lax.dot_general(k, q, last, preferred_element_type=f32)
        scores = scores.reshape(lines, TILE, tok) * (scale * math.log2(math.e))
        scores = (scores + bias[0:lines, :][:, None, :]).reshape(rows, tok)
        raised = jnp.exp2(scores - jnp.max(scores, axis=0, keepdims=True))
        weights = raised * (1.0 / jnp.sum(raised, axis=0, keepdims=True))
        weights_b = weights.astype(jnp.bfloat16)
        out = lax.dot_general(v, weights_b, first, preferred_element_type=f32)
        out_b = out.T.astype(jnp.bfloat16)
        o_ref[:, narrow] = out_b
        out_t = out.astype(jnp.bfloat16).astype(f32)
        delta = jnp.sum(g.astype(f32).T * out_t, axis=0, keepdims=True)
        dweights = lax.dot_general(v, g, last, preferred_element_type=f32)
        dscores = (weights * (dweights - delta)).astype(jnp.bfloat16)
        dq = lax.dot_general(k, dscores, first, preferred_element_type=f32) * scale
        dq_ref[:, narrow] = dq.T.astype(jnp.bfloat16)
        dk = jnp.dot(dscores, q, preferred_element_type=f32) * scale
        dv = jnp.dot(weights_b, g, preferred_element_type=f32)
        own[:, k_cols] = dk[:tok]
        own[:, v_cols] = dv[:tok]
        gsend[:, k_cols] = dk[tok:].astype(jnp.bfloat16)
        gsend[:, v_cols] = dv[tok:].astype(jnp.bfloat16)
        return carry

    def piece(c, i):
        return pl.ds(pl.multiple_of(c * width + i * D_HEAD, D_HEAD), D_HEAD)

    def fold(c):
        @pl.when(cuts)
        def _():
            fold_recv(c).wait_recv()
            for i in range(2 * chunk):
                extra = folded[:, piece(c, i)].astype(jnp.float32)
                add_tile(gsend, odd * tok, extra, cut_mark, piece(c, i))

        @pl.when(cuts & passer)
        def _():
            fold_send_pass(c).start()

        @pl.when(cuts & jnp.logical_not(passer))
        def _():
            fold_send(c).start()

    def join(c):
        @pl.when(passes & passer)
        def _():
            join_recv(c).wait_recv()

        @pl.when(passes & jnp.logical_not(passer))
        def _():
            back2_recv(c).wait_recv()

        @pl.when(goes_on)
        def _():
            back8_recv(c).wait_recv()

        @pl.when(passes)
        def _():
            row = pl.multiple_of(2 * tok + (2 + pass_slot) * TILE, TILE)
            f32 = jnp.float32
            for i in range(2 * chunk):
                cols = piece(c, i)
                kept = gsend[pl.ds(row, TILE), cols].astype(f32)
                read8, read2 = back8[:, cols].astype(f32), back2[:, cols].astype(f32)
                for t in range(tiles):
                    at = pl.ds(t * TILE, TILE)
                    total = joined[at, cols].astype(f32)
                    for j, part in ((keep_mark, kept), (on_mark, read8), (turn_mark, read2)):
                        total = total + (marks[pl.ds(j, 1), :] == float(t)).astype(f32) * part
                    joined[at, cols] = total.astype(joined.dtype)
            join_send(c).start()

    def work(c, carry):
        @pl.when(c + lead < chunks)
        def _():
            push(c + lead, 0)

        @pl.when(passes)
        def _():
            pass_recv(c).wait_recv()

        @pl.when(passes & passer)
        def _():
            pass_send(c).start()

        @pl.when(goes_on)
        def _():
            for i in range(2 * chunk):
                onward[:, piece(c, i)] = pick(passed, on_mark, piece(c, i))
            on_send(c).start()

        @pl.when(passes & jnp.logical_not(passer))
        def _():
            for i in range(2 * chunk):
                turned[:, piece(c, i)] = pick(passed, turn_mark, piece(c, i))
            turn_send(c).start()

        @pl.when(passes)
        def _():
            row = pl.multiple_of(3 * tok + (2 + pass_slot) * TILE, TILE)
            for i in range(2 * chunk):
                kv[pl.ds(row, TILE), piece(c, i)] = pick(passed, keep_mark, piece(c, i))

        @pl.when(cuts)
        def _():
            whole_recv(c).wait_recv()
            for i in range(2 * chunk):
                cut[:, piece(c, i)] = pick(kv, cut_mark, piece(c, i), tok * (1 + odd))
            cut_send(c).start()

        for s in order:
            @pl.when(key_in(s))
            def _():
                key_recv(s, c).wait_recv()

        lax.fori_loop(c * chunk, (c + 1) * chunk, head, 0)
        for s in order:
            send_grad(s, c, lambda copy: copy.start())

        @pl.when(c >= 1)
        def _():
            fold(c - 1)

        @pl.when(c >= 2)
        def _():
            join(c - 2)
        return carry

    lax.fori_loop(0, chunks, work, 0)
    fold(chunks - 1)
    if chunks > 1:
        join(chunks - 2)
    join(chunks - 1)

    for d, row, count in slots:
        @pl.when(jnp.logical_not(grad_in(slots.index((d, row, count)))))
        def _():
            grecv[pl.ds(row - tok, count), :] = jnp.zeros((count, grecv.shape[1]), grecv.dtype)

    def gather(c, carry):
        for s in order:
            @pl.when(grad_in(s))
            def _():
                grad_recv(s, c).wait_recv()

        @pl.when(starts)
        def _():
            back_recv(c).wait_recv()

        for i in range(chunk):
            h = c * chunk + i
            narrow = pl.ds(pl.multiple_of(h * D_HEAD, D_HEAD), D_HEAD)
            for part, ref in ((0, dk_ref), (1, dv_ref)):
                cols = pl.ds(pl.multiple_of(h * 2 * D_HEAD + part * D_HEAD, D_HEAD), D_HEAD)
                for t in range(tiles):
                    at = pl.ds(t * TILE, TILE)
                    total = own[at, cols] + back[at, cols].astype(jnp.float32)
                    for _, row, _ in slots[:2]:
                        total = total + grecv[pl.ds(row - tok + t * TILE, TILE), cols].astype(
                            jnp.float32
                        )
                    for j, (_, row, _) in enumerate(slots[2:]):
                        here = (marks[pl.ds(j, 1), :] == float(t)).astype(jnp.float32)
                        total = total + here * grecv[pl.ds(row - tok, TILE), cols].astype(
                            jnp.float32
                        )
                    ref[at, narrow] = total.astype(jnp.bfloat16)
        return carry

    lax.fori_loop(0, chunks, gather, 0)

    def drain(c, carry):
        for s in order:
            @pl.when(key_out(s))
            def _():
                key_send(s, c).wait_send()

            send_grad(s, c, lambda copy: copy.wait_send())

        @pl.when(starts)
        def _():
            start_send(c).wait_send()

        @pl.when(passes)
        def _():
            join_send(c).wait_send()

        @pl.when(passes & passer)
        def _():
            pass_send(c).wait_send()

        @pl.when(passes & jnp.logical_not(passer))
        def _():
            turn_send(c).wait_send()

        @pl.when(goes_on)
        def _():
            on_send(c).wait_send()

        @pl.when(cuts)
        def _():
            cut_send(c).wait_send()

        @pl.when(cuts & passer)
        def _():
            fold_send_pass(c).wait_send()

        @pl.when(cuts & jnp.logical_not(passer))
        def _():
            fold_send(c).wait_send()
        return carry

    lax.fori_loop(0, chunks, drain, 0)


def per_device(queries, keys_in, values_in, out_grad, band_mask, far_tiles):
    tok, cols = queries.shape
    heads = cols // D_HEAD
    n = lax.axis_size("tm")
    chunk = 3 if heads % 3 == 0 else 1
    chunks = heads // chunk
    slots = 2 + len(far_strides(n))
    rows = 3 * tok + (slots - 2) * TILE
    lines = -(-rows // TILE // 8) * 8
    flops = 2 * 6 * tok * rows * cols
    bf16 = jnp.bfloat16
    vmem = pl.BlockSpec(memory_space=pltpu.VMEM)
    out = jax.ShapeDtypeStruct((tok, cols), bf16)
    sems = pltpu.SemaphoreType.DMA((slots, chunks))
    return pl.pallas_call(
        functools.partial(kernel, n, chunk),
        out_shape=(out,) * 4,
        in_specs=[vmem] * 6,
        out_specs=(vmem,) * 4,
        scratch_shapes=[
            pltpu.VMEM((rows, 2 * cols), bf16),
            pltpu.VMEM((rows - 3 * tok, 2 * cols), bf16),
            pltpu.VMEM((lines, tok), jnp.float32),
            pltpu.VMEM((16, D_HEAD), jnp.float32),
            pltpu.VMEM((tok, 2 * cols), jnp.float32),
            pltpu.VMEM((rows - tok, 2 * cols), bf16),
            pltpu.VMEM((rows - tok, 2 * cols), bf16),
            pltpu.VMEM((tok, 2 * cols), bf16),
            pltpu.VMEM((TILE, 2 * cols), bf16),
            pltpu.VMEM((TILE, 2 * cols), bf16),
            pltpu.VMEM((tok, 2 * cols), bf16),
            pltpu.VMEM((TILE, 2 * cols), bf16),
            pltpu.VMEM((TILE, 2 * cols), bf16),
            pltpu.VMEM((TILE, 2 * cols), bf16),
            pltpu.VMEM((TILE, 2 * cols), bf16),
            pltpu.VMEM((tok, 2 * cols), bf16),
            sems, sems, sems, sems,
            pltpu.SemaphoreType.DMA((6, chunks)),
            pltpu.SemaphoreType.DMA((6, chunks)),
        ],
        compiler_params=pltpu.CompilerParams(
            collective_id=0, has_side_effects=True, vmem_limit_bytes=60 * 1024 * 1024
        ),
        cost_estimate=pl.CostEstimate(
            flops=flops, bytes_accessed=16 * tok * cols, transcendentals=tok * rows * heads
        ),
    )(queries, keys_in, values_in, out_grad, band_mask, far_tiles)


def solution(mesh):
    cells = P(("group", "tm"), ("head", "sub"))
    return jax.shard_map(
        per_device,
        mesh=mesh,
        in_specs=(cells,) * 4 + (P("tm", None), P()),
        out_specs=(cells,) * 4,
        check_vma=False,
    )
```

```python
import functools
import math

import jax
import jax.numpy as jnp
from jax import lax
from jax.experimental import pallas as pl
from jax.experimental.pallas import tpu as pltpu
from jax.sharding import PartitionSpec as P

D_HEAD = 128
TILE = 128
LEAD = 12
MESH = pl.DeviceIdType.MESH


def far_strides(count):
    strides = []
    stride = 2
    while stride < count:
        strides += [stride, -stride]
        stride *= 2
    return strides


def kernel(
    n, chunk, q_ref, k_ref, v_ref, g_ref, band_ref, far_ref, o_ref, dq_ref, dk_ref, dv_ref,
    kv, picked, bias, marks, own, gsend, grecv, passed, cut, folded, joined,
    send_sem, recv_sem, gsend_sem, grecv_sem, xsend_sem, xrecv_sem,
):
    tok, cols_all = q_ref.shape
    heads = cols_all // D_HEAD
    chunks = heads // chunk
    lead = min(LEAD, chunks)
    width = 2 * D_HEAD * chunk
    tiles = tok // TILE
    rows = kv.shape[0]
    pos = lax.axis_index("tm")
    scale = 1.0 / math.sqrt(D_HEAD)
    far = far_strides(n)
    slots = [(1, tok, tok), (-1, 2 * tok, tok)]
    slots += [(d, 3 * tok + j * TILE, TILE) for j, d in enumerate(far)]
    order = list(range(len(slots)))[::-1]

    def within(index):
        return (index >= 0) & (index < n)

    odd = lax.rem(pos, 2)
    side = 1 - 2 * odd
    mate = pos + side
    cuts = within(pos - side)
    quarter = lax.rem(pos, 4)
    third, zeroth = quarter == 3, quarter == 0
    ahead = jnp.where(third, 1, -1)
    passer = third | zeroth
    passes = passer & within(pos - 4 * ahead)
    starts = passer & within(pos + 4 * ahead)
    pass_slot = jnp.where(third, 0, 1)
    cut_mark, keep_mark = len(far), len(far) + 1
    direct = [
        jnp.logical_not(third), jnp.logical_not(zeroth), odd == 0, odd == 1,
        jnp.logical_not(third), jnp.logical_not(zeroth),
    ]
    direct += [jnp.bool_(True)] * (len(slots) - 6)

    def key_out(s):
        return within(pos + slots[s][0]) & direct[s]

    def key_in(s):
        live = within(pos - slots[s][0])
        if s < 2:
            return live & (odd == 1 - s)
        return live & direct[s] if s in (4, 5) else live

    def grad_out(s):
        live = within(pos - slots[s][0])
        if s < 2:
            return live & (odd == 1 - s)
        return live & direct[s] if s in (4, 5) else live

    def grad_in(s):
        live = within(pos + slots[s][0])
        return live if s < 2 else live & direct[s]

    barrier = pltpu.get_barrier_semaphore()
    partners = jnp.int32(0)
    for d in [d for d, _, _ in slots] + [3, -3]:
        partners = partners + within(pos + d).astype(jnp.int32)

        @pl.when(within(pos + d))
        def _():
            pl.semaphore_signal(barrier, inc=1, device_id={"tm": pos + d}, device_id_type=MESH)

    pl.semaphore_wait(barrier, partners)

    def span(c):
        return pl.ds(pl.multiple_of(c * width, 2 * D_HEAD), width)

    def key_send(s, c):
        d, row, count = slots[s]
        if s < 2:
            src = kv.at[pl.ds(0, tok), span(c)]
        else:
            src = picked.at[pl.ds((s - 2) * TILE, TILE), span(c)]
        return pltpu.make_async_remote_copy(
            src_ref=src, dst_ref=kv.at[pl.ds(row, count), span(c)],
            send_sem=send_sem.at[s, c], recv_sem=recv_sem.at[s, c],
            device_id={"tm": pos + d}, device_id_type=MESH,
        )

    def key_recv(s, c):
        d, row, count = slots[s]
        ref = kv.at[pl.ds(row, count), span(c)]
        return pltpu.make_async_remote_copy(
            src_ref=ref, dst_ref=ref, send_sem=send_sem.at[s, c], recv_sem=recv_sem.at[s, c],
            device_id={"tm": pos - d}, device_id_type=MESH,
        )

    def remote(src, dst, sent, arrived, to):
        return pltpu.make_async_remote_copy(
            src_ref=src, dst_ref=dst, send_sem=sent, recv_sem=arrived,
            device_id={"tm": to}, device_id_type=MESH,
        )

    def start_send(c):
        return remote(
            kv.at[pl.ds(0, tok), span(c)], passed.at[:, span(c)],
            xsend_sem.at[3, c], xrecv_sem.at[0, c], pos + 4 * ahead,
        )

    def pass_recv(c):
        ref = passed.at[:, span(c)]
        return remote(ref, ref, xsend_sem.at[3, c], xrecv_sem.at[0, c], pos - 4 * ahead)

    def pass_send(c):
        row = pl.multiple_of(tok * (1 + pass_slot), tok)
        return remote(
            passed.at[:, span(c)], kv.at[pl.ds(row, tok), span(c)],
            xsend_sem.at[0, c], recv_sem.at[pass_slot, c], pos - 3 * ahead,
        )

    def whole_recv(c):
        ref = kv.at[pl.ds(pl.multiple_of(tok * (1 + odd), tok), tok), span(c)]
        return remote(ref, ref, send_sem.at[odd, c], recv_sem.at[odd, c], pos - side)

    def cut_send(c):
        row = pl.multiple_of(3 * tok + odd * TILE, TILE)
        return remote(
            cut.at[:, span(c)], kv.at[pl.ds(row, TILE), span(c)],
            xsend_sem.at[1, c], recv_sem.at[2 + odd, c], mate,
        )

    def fold_recv(c):
        ref = folded.at[:, span(c)]
        return remote(ref, ref, xsend_sem.at[1, c], xrecv_sem.at[1, c], mate)

    def whole_rows():
        return pl.ds(pl.multiple_of(odd * tok, tok), tok)

    def fold_send(c):
        return remote(
            gsend.at[whole_rows(), span(c)], grecv.at[whole_rows(), span(c)],
            gsend_sem.at[odd, c], grecv_sem.at[odd, c], pos - side,
        )

    def fold_send_pass(c):
        return remote(
            gsend.at[whole_rows(), span(c)], joined.at[:, span(c)],
            gsend_sem.at[odd, c], xrecv_sem.at[2, c], pos + 3 * side,
        )

    def join_recv(c):
        ref = joined.at[:, span(c)]
        return remote(ref, ref, xsend_sem.at[2, c], xrecv_sem.at[2, c], pos - 3 * ahead)

    def join_send(c):
        row = pl.multiple_of(tok * pass_slot, tok)
        return remote(
            joined.at[:, span(c)], grecv.at[pl.ds(row, tok), span(c)],
            xsend_sem.at[2, c], grecv_sem.at[pass_slot, c], pos - 4 * ahead,
        )

    def grad_send(s, c):
        d, row, count = slots[s]
        src = gsend.at[pl.ds(row - tok, count), span(c)]
        return remote(
            src, grecv.at[pl.ds(row - tok, count), span(c)],
            gsend_sem.at[s, c], grecv_sem.at[s, c], pos - d,
        )

    def mate_send(s, c):
        d, row, count = slots[s]
        src = gsend.at[pl.ds(row - tok, count), span(c)]
        return remote(
            src, folded.at[:, span(c)], gsend_sem.at[s, c], xrecv_sem.at[1, c], mate
        )

    def send_grad(s, c, action):
        if s in (2, 3):
            to_mate = odd == 3 - s

            @pl.when(grad_out(s) & to_mate)
            def _():
                action(mate_send(s, c))

            @pl.when(grad_out(s) & jnp.logical_not(to_mate))
            def _():
                action(grad_send(s, c))
        else:
            @pl.when(grad_out(s))
            def _():
                action(grad_send(s, c))

    def grad_recv(s, c):
        d, row, count = slots[s]
        ref = grecv.at[pl.ds(row - tok, count), span(c)]
        return pltpu.make_async_remote_copy(
            src_ref=ref, dst_ref=ref, send_sem=gsend_sem.at[s, c], recv_sem=grecv_sem.at[s, c],
            device_id={"tm": pos + d}, device_id_type=MESH,
        )

    def far_entry(reader, source):
        line = far_ref[pl.ds(jnp.clip(reader, 0, n - 1), 1), :].astype(jnp.float32)
        here = lax.broadcasted_iota(jnp.int32, line.shape, 1) == jnp.clip(source, 0, n - 1)
        return jnp.sum(jnp.where(here, line, 0.0), axis=1, keepdims=True)

    for j, d in enumerate(far):
        marks[pl.ds(j, 1), :] = jnp.broadcast_to(far_entry(pos + d, pos), (1, D_HEAD))

    marks[pl.ds(cut_mark, 1), :] = jnp.broadcast_to(
        far_entry(mate, pos - side), (1, D_HEAD)
    )
    marks[pl.ds(keep_mark, 1), :] = jnp.broadcast_to(
        far_entry(pos, pos - 4 * ahead), (1, D_HEAD)
    )

    def pick(ref, j, cols, base=0):
        out = None
        for t in range(tiles):
            row = base + t * TILE
            if not isinstance(row, int):
                row = pl.multiple_of(row, TILE)
            part = ref[pl.ds(row, TILE), cols].astype(jnp.float32)
            here = jnp.broadcast_to(marks[pl.ds(j, 1), :], (TILE, D_HEAD)) == float(t)
            out = part if out is None else jnp.where(here, part, out)
        return out.astype(ref.dtype)

    def add_tile(ref, base, extra, j, cols):
        for t in range(tiles):
            row = base + t * TILE
            if not isinstance(row, int):
                row = pl.multiple_of(row, TILE)
            here = (marks[pl.ds(j, 1), :] == float(t)).astype(jnp.float32)
            total = ref[pl.ds(row, TILE), cols].astype(jnp.float32) + here * extra
            ref[pl.ds(row, TILE), cols] = total.astype(ref.dtype)

    def push(c, carry):
        for i in range(chunk):
            h = c * chunk + i
            narrow = pl.ds(pl.multiple_of(h * D_HEAD, D_HEAD), D_HEAD)
            k_cols = pl.ds(pl.multiple_of(h * 2 * D_HEAD, D_HEAD), D_HEAD)
            v_cols = pl.ds(pl.multiple_of(h * 2 * D_HEAD + D_HEAD, D_HEAD), D_HEAD)
            for j, d in enumerate(far):
                picked[pl.ds(j * TILE, TILE), k_cols] = pick(k_ref, j, narrow)
                picked[pl.ds(j * TILE, TILE), v_cols] = pick(v_ref, j, narrow)
            kv[pl.ds(0, tok), k_cols] = k_ref[:, narrow]
            kv[pl.ds(0, tok), v_cols] = v_ref[:, narrow]
        @pl.when(starts)
        def _():
            start_send(c).start()

        for s in order:
            @pl.when(key_out(s))
            def _():
                key_send(s, c).start()
        return carry

    lax.fori_loop(0, lead, push, 0)

    for d, row, count in slots:
        @pl.when(jnp.logical_not(within(pos - d)))
        def _():
            kv[pl.ds(row, count), :] = jnp.zeros((count, kv.shape[1]), kv.dtype)

    lane = lax.broadcasted_iota(jnp.int32, (1, tok), 1) // TILE

    for t in range(rows // TILE):
        if t < 3 * tiles:
            block = t // tiles
            shift = (0, -1, 1)[block]
            at = t % tiles
            window = tiles * (1 + shift) + at
            times = jnp.zeros((1, tok), jnp.float32)
            for a in range(tiles):
                on = (band_ref[a : a + 1, window : window + 1] != 0).astype(jnp.float32)
                times = jnp.where(lane == a, jnp.broadcast_to(on, (1, tok)), times)
            if block:
                extra = (far_entry(pos, pos + shift) == float(at)).astype(jnp.float32)
                times = times + jnp.broadcast_to(extra, (1, tok))
        else:
            shift = -far[t - 3 * tiles]
            times = jnp.ones((1, tok), jnp.float32)
        times = times * within(pos + shift).astype(jnp.float32)
        bias[pl.ds(t, 1), :] = jnp.where(times == 0.0, -1e30, times - 1.0)

    lines = rows // TILE

    def head(h, carry):
        narrow = pl.ds(pl.multiple_of(h * D_HEAD, D_HEAD), D_HEAD)
        k_cols = pl.ds(pl.multiple_of(h * 2 * D_HEAD, D_HEAD), D_HEAD)
        v_cols = pl.ds(pl.multiple_of(h * 2 * D_HEAD + D_HEAD, D_HEAD), D_HEAD)
        q, g = q_ref[:, narrow], g_ref[:, narrow]
        k, v = kv[:, k_cols], kv[:, v_cols]
        last = (((1,), (1,)), ((), ()))
        first = (((0,), (0,)), ((), ()))
        f32 = jnp.float32
        scores = lax.dot_general(k, q, last, preferred_element_type=f32)
        scores = scores.reshape(lines, TILE, tok) * (scale * math.log2(math.e))
        scores = (scores + bias[0:lines, :][:, None, :]).reshape(rows, tok)
        raised = jnp.exp2(scores - jnp.max(scores, axis=0, keepdims=True))
        weights = raised * (1.0 / jnp.sum(raised, axis=0, keepdims=True))
        weights_b = weights.astype(jnp.bfloat16)
        out = lax.dot_general(v, weights_b, first, preferred_element_type=f32)
        out_b = out.T.astype(jnp.bfloat16)
        o_ref[:, narrow] = out_b
        out_t = out.astype(jnp.bfloat16).astype(f32)
        delta = jnp.sum(g.astype(f32).T * out_t, axis=0, keepdims=True)
        dweights = lax.dot_general(v, g, last, preferred_element_type=f32)
        dscores = (weights * (dweights - delta)).astype(jnp.bfloat16)
        dq = lax.dot_general(k, dscores, first, preferred_element_type=f32) * scale
        dq_ref[:, narrow] = dq.T.astype(jnp.bfloat16)
        dk = jnp.dot(dscores, q, preferred_element_type=f32) * scale
        dv = jnp.dot(weights_b, g, preferred_element_type=f32)
        own[:, k_cols] = dk[:tok]
        own[:, v_cols] = dv[:tok]
        gsend[:, k_cols] = dk[tok:].astype(jnp.bfloat16)
        gsend[:, v_cols] = dv[tok:].astype(jnp.bfloat16)
        return carry

    def piece(c, i):
        return pl.ds(pl.multiple_of(c * width + i * D_HEAD, D_HEAD), D_HEAD)

    def fold(c):
        @pl.when(cuts)
        def _():
            fold_recv(c).wait_recv()
            for i in range(2 * chunk):
                extra = folded[:, piece(c, i)].astype(jnp.float32)
                add_tile(gsend, odd * tok, extra, cut_mark, piece(c, i))

        @pl.when(cuts & passer)
        def _():
            fold_send_pass(c).start()

        @pl.when(cuts & jnp.logical_not(passer))
        def _():
            fold_send(c).start()

    def join(c):
        @pl.when(passes)
        def _():
            join_recv(c).wait_recv()
            row = pl.multiple_of(2 * tok + (2 + pass_slot) * TILE, TILE)
            for i in range(2 * chunk):
                extra = gsend[pl.ds(row, TILE), piece(c, i)].astype(jnp.float32)
                add_tile(joined, 0, extra, keep_mark, piece(c, i))
            join_send(c).start()

    def work(c, carry):
        @pl.when(c + lead < chunks)
        def _():
            push(c + lead, 0)

        @pl.when(passes)
        def _():
            pass_recv(c).wait_recv()
            pass_send(c).start()
            row = pl.multiple_of(3 * tok + (2 + pass_slot) * TILE, TILE)
            for i in range(2 * chunk):
                kv[pl.ds(row, TILE), piece(c, i)] = pick(passed, keep_mark, piece(c, i))

        @pl.when(cuts)
        def _():
            whole_recv(c).wait_recv()
            for i in range(2 * chunk):
                cut[:, piece(c, i)] = pick(kv, cut_mark, piece(c, i), tok * (1 + odd))
            cut_send(c).start()

        for s in order:
            @pl.when(key_in(s))
            def _():
                key_recv(s, c).wait_recv()

        lax.fori_loop(c * chunk, (c + 1) * chunk, head, 0)
        for s in order:
            send_grad(s, c, lambda copy: copy.start())

        @pl.when(c >= 1)
        def _():
            fold(c - 1)

        @pl.when(c >= 2)
        def _():
            join(c - 2)
        return carry

    lax.fori_loop(0, chunks, work, 0)
    fold(chunks - 1)
    if chunks > 1:
        join(chunks - 2)
    join(chunks - 1)

    for d, row, count in slots:
        @pl.when(jnp.logical_not(grad_in(slots.index((d, row, count)))))
        def _():
            grecv[pl.ds(row - tok, count), :] = jnp.zeros((count, grecv.shape[1]), grecv.dtype)

    def gather(c, carry):
        for s in order:
            @pl.when(grad_in(s))
            def _():
                grad_recv(s, c).wait_recv()

        for i in range(chunk):
            h = c * chunk + i
            narrow = pl.ds(pl.multiple_of(h * D_HEAD, D_HEAD), D_HEAD)
            for part, ref in ((0, dk_ref), (1, dv_ref)):
                cols = pl.ds(pl.multiple_of(h * 2 * D_HEAD + part * D_HEAD, D_HEAD), D_HEAD)
                for t in range(tiles):
                    at = pl.ds(t * TILE, TILE)
                    total = own[at, cols]
                    for _, row, _ in slots[:2]:
                        total = total + grecv[pl.ds(row - tok + t * TILE, TILE), cols].astype(
                            jnp.float32
                        )
                    for j, (_, row, _) in enumerate(slots[2:]):
                        here = (marks[pl.ds(j, 1), :] == float(t)).astype(jnp.float32)
                        total = total + here * grecv[pl.ds(row - tok, TILE), cols].astype(
                            jnp.float32
                        )
                    ref[at, narrow] = total.astype(jnp.bfloat16)
        return carry

    lax.fori_loop(0, chunks, gather, 0)

    def drain(c, carry):
        for s in order:
            @pl.when(key_out(s))
            def _():
                key_send(s, c).wait_send()

            send_grad(s, c, lambda copy: copy.wait_send())

        @pl.when(starts)
        def _():
            start_send(c).wait_send()

        @pl.when(passes)
        def _():
            pass_send(c).wait_send()
            join_send(c).wait_send()

        @pl.when(cuts)
        def _():
            cut_send(c).wait_send()

        @pl.when(cuts & passer)
        def _():
            fold_send_pass(c).wait_send()

        @pl.when(cuts & jnp.logical_not(passer))
        def _():
            fold_send(c).wait_send()
        return carry

    lax.fori_loop(0, chunks, drain, 0)


def per_device(queries, keys_in, values_in, out_grad, band_mask, far_tiles):
    tok, cols = queries.shape
    heads = cols // D_HEAD
    n = lax.axis_size("tm")
    chunk = 3 if heads % 3 == 0 else 1
    chunks = heads // chunk
    slots = 2 + len(far_strides(n))
    rows = 3 * tok + (slots - 2) * TILE
    lines = -(-rows // TILE // 8) * 8
    flops = 2 * 6 * tok * rows * cols
    bf16 = jnp.bfloat16
    vmem = pl.BlockSpec(memory_space=pltpu.VMEM)
    out = jax.ShapeDtypeStruct((tok, cols), bf16)
    sems = pltpu.SemaphoreType.DMA((slots, chunks))
    return pl.pallas_call(
        functools.partial(kernel, n, chunk),
        out_shape=(out,) * 4,
        in_specs=[vmem] * 6,
        out_specs=(vmem,) * 4,
        scratch_shapes=[
            pltpu.VMEM((rows, 2 * cols), bf16),
            pltpu.VMEM((rows - 3 * tok, 2 * cols), bf16),
            pltpu.VMEM((lines, tok), jnp.float32),
            pltpu.VMEM((16, D_HEAD), jnp.float32),
            pltpu.VMEM((tok, 2 * cols), jnp.float32),
            pltpu.VMEM((rows - tok, 2 * cols), bf16),
            pltpu.VMEM((rows - tok, 2 * cols), bf16),
            pltpu.VMEM((tok, 2 * cols), bf16),
            pltpu.VMEM((TILE, 2 * cols), bf16),
            pltpu.VMEM((TILE, 2 * cols), bf16),
            pltpu.VMEM((tok, 2 * cols), bf16),
            sems, sems, sems, sems,
            pltpu.SemaphoreType.DMA((4, chunks)),
            pltpu.SemaphoreType.DMA((3, chunks)),
        ],
        compiler_params=pltpu.CompilerParams(
            collective_id=0, has_side_effects=True, vmem_limit_bytes=60 * 1024 * 1024
        ),
        cost_estimate=pl.CostEstimate(
            flops=flops, bytes_accessed=16 * tok * cols, transcendentals=tok * rows * heads
        ),
    )(queries, keys_in, values_in, out_grad, band_mask, far_tiles)


def solution(mesh):
    cells = P(("group", "tm"), ("head", "sub"))
    return jax.shard_map(
        per_device,
        mesh=mesh,
        in_specs=(cells,) * 4 + (P("tm", None), P()),
        out_specs=(cells,) * 4,
        check_vma=False,
    )
```
